32 devices in a mesh: node: 4 (over y, x), freq: 8 (over z, core).
Axes of the slice: x: 2, y: 2, z: 4, core: 2. Of those that a mesh axis runs over, the one named last changes fastest.
Arguments:
- first_vector: float32 [2, 256, 512, 256], P(None, 'freq', 'node'), may hold values from -6 to 6
- second_vector: float32 [2, 256, 512, 256], P(None, 'freq', 'node'), may hold values from -6 to 6
- conductance: float32 [2, 256, 512, 256], P(None, 'freq', 'node'), may hold values from 0.1 to 2
- terminals: int32 [512, 3], replicated, may hold values from 0 to 127
- pattern: int32 [16, 3], P('node'), may hold values from 0 to 3, all different within a row
- conduct_blocks: float32 [16, 3, 32, 32], P('node'), may hold values from -0.625 to 0.625
- capacit_blocks: float32 [16, 3, 32, 32], P('node'), may hold values from -0.625 to 0.625
Outputs:
- first_product: float32 [2, 256, 512, 256], P(None, 'freq', 'node')
- second_product: float32 [2, 256, 512, 256], P(None, 'freq', 'node')
The draws below stay inside these ranges and needn't reach their ends.
Inputs may be any that keep to these rules, and one draw needn't show every extreme that they name: `terminals`: drain and source indices count within the transistor's own node block; transistor j of a node block (j counted within the block) takes its gate from node block j // 32, so every node block draws exactly 32 gates from every node block. `pattern`: each row names 3 different column blocks, counted within the row's own node block.
All inputs are finite; a program needn't handle non-finite values.
Results may differ from the reference program's by a relative error of at most 0.000058.
Values sent between devices are 32-bit elements; how exact they have to be, the bound alone decides.
A program may use at most 192 MiB of HBM per device.

```python
import math
import jax
import jax.numpy as jnp
from jax import lax

NODE_DEV = 128
OUTER = 256
INNER = 256
BS = 32
NNZ = 3
NODES = 512
BLOCKS = 16
N_NODE = 4


def plant(values, stream_key, least, largest):
    longest = values.shape.index(max(values.shape))
    spots = []
    for shift in (0, 1):
        where = [jax.random.randint(jax.random.fold_in(stream_key, axis), (), 0, length) for axis, length in enumerate(values.shape)]
        where[longest] = (where[longest] + shift) % values.shape[longest]
        spots.append(tuple(where))
    return values.at[spots[0]].set(least).at[spots[1]].set(largest)


def steps_of(own_key, shape, pieces, smallest, largest):
    loudness, own = 1.0, jax.random.fold_in(own_key, 6)
    for axis_at, shards_of in pieces:
        draws = jnp.exp(jax.random.uniform(jax.random.fold_in(own, axis_at), (shards_of,), jnp.float32, smallest / len(pieces), largest / len(pieces)))
        loudness = loudness * jnp.repeat(draws, shape[axis_at] // shards_of).reshape([-1 if axis == axis_at else 1 for axis in range(len(shape))])
    return loudness


def choose_distinct(key, rows, amount, top, lift):
    order = jax.random.permutation(jax.random.fold_in(key, 1), amount)
    favour = order
    for power in range(3):
        favour = favour * favour // amount
    favour = favour * lift // amount
    chance = jax.random.randint(jax.random.fold_in(key, 2), (rows, amount), 0, 4096) + favour
    sure = jax.random.permutation(jax.random.fold_in(key, 3), rows)[jnp.arange(amount) % rows]
    chance = jnp.where(jnp.arange(rows)[:, None] == sure[None, :], 1 << 14, chance)
    priority = chance * amount + jnp.arange(amount)
    return lax.top_k(priority.astype(jnp.int32), top)[1].astype(jnp.int32)


def centred(rng, shape, width, bound, cuts=(), held_as=jnp.bfloat16):
    level = steps_of(rng, shape, cuts, -0.22, 0.18) if cuts else 1.0
    values = jax.random.normal(rng, shape, jnp.float32) * width * level
    return jnp.minimum(jnp.maximum(values, -bound), bound).astype(held_as)


def setup_inputs(seed: int = 0) -> dict:
    arg_keys = jax.random.split(jax.random.key(seed), 8)
    first_vector = centred(arg_keys[0], (2, OUTER, NODES, INNER), 1.0, 6.0, ((1, 8), (2, 4)), jnp.float32)
    second_vector = centred(arg_keys[1], (2, OUTER, NODES, INNER), 1.0, 6.0, ((1, 8), (2, 4)), jnp.float32)
    conductance = jnp.clip(jnp.exp(math.log(2.0) - 2.9957323 * jax.random.uniform(arg_keys[2], (2, INNER, NODES, OUTER), jnp.float32) ** steps_of(arg_keys[2], (2, INNER, NODES, OUTER), ((1, 8), (2, 4)), -0.2, 0.2)), 0.1, 2.0)
    terminals = plant(jax.random.randint(arg_keys[3], (NODES, 3), 0, NODE_DEV), jax.random.fold_in(arg_keys[3], 1), 0, NODE_DEV - 1).astype(jnp.int32)
    pattern = choose_distinct(arg_keys[4], BLOCKS, NODE_DEV // BS, NNZ, 0)
    conduct_blocks = centred(arg_keys[5], (BLOCKS, NNZ, BS, BS), (NNZ * BS) ** -0.5, 0.625, ((0, 4),), jnp.float32)
    capacit_blocks = centred(arg_keys[6], (BLOCKS, NNZ, BS, BS), (NNZ * BS) ** -0.5, 0.625, ((0, 4),), jnp.float32)
    return dict(first_vector=first_vector, second_vector=second_vector, conductance=conductance, terminals=terminals, pattern=pattern, conduct_blocks=conduct_blocks, capacit_blocks=capacit_blocks)


def reference(first_vector, second_vector, conductance, terminals, pattern, conduct_blocks, capacit_blocks):
    node_dev = NODE_DEV
    nodes = NODES
    samples = OUTER * INNER
    capacity = node_dev // N_NODE
    block_count = node_dev // BS
    device = jnp.arange(nodes, dtype=jnp.int32)
    group = device // node_dev
    slot = device % node_dev
    drain = group * node_dev + terminals[:, 0]
    source = group * node_dev + terminals[:, 1]
    gate = (slot // capacity) * node_dev + terminals[:, 2]
    trans_g = conductance[0].transpose(1, 2, 0).reshape(nodes, samples)
    output_g = conductance[1].transpose(1, 2, 0).reshape(nodes, samples)
    pattern_hot = (pattern[:, :, None] == jnp.arange(block_count, dtype=jnp.int32)[None, None, :]).astype(jnp.float32)
    conduct_dense = jnp.einsum("bjc,bjrs->brcs", pattern_hot, conduct_blocks, precision=lax.Precision.HIGHEST)
    conduct_dense = conduct_dense.reshape(N_NODE, node_dev, node_dev)
    capacit_dense = jnp.einsum("bjc,bjrs->brcs", pattern_hot, capacit_blocks, precision=lax.Precision.HIGHEST)
    capacit_dense = capacit_dense.reshape(N_NODE, node_dev, node_dev)
    bins = jnp.arange(samples, dtype=jnp.int32)
    signed = jnp.where(bins < samples // 2, bins, bins - samples)
    angular = (signed.astype(jnp.float32) * (2.0 * math.pi / samples)).reshape(INNER, OUTER).T[:, None, :]

    def apply_mna(dense, part):
        grouped = part.reshape(OUTER, N_NODE, node_dev, INNER)
        result = jnp.einsum("grs,agsb->agrb", dense, grouped, precision=lax.Precision.HIGHEST)
        return result.reshape(OUTER, nodes, INNER)

    def product(vector):
        spectrum = lax.complex(vector[0], vector[1]).transpose(1, 2, 0).reshape(nodes, samples)
        signal = jnp.fft.ifft(spectrum, axis=1)
        current = trans_g * (signal[gate] - signal[source]) + output_g * (signal[drain] - signal[source])
        injected = jnp.zeros_like(signal).at[drain].add(current).at[source].add(-current)
        response = jnp.fft.fft(injected, axis=1).reshape(nodes, INNER, OUTER).transpose(2, 0, 1)
        real_out = apply_mna(conduct_dense, vector[0]) - angular * apply_mna(capacit_dense, vector[1]) + jnp.real(response)
        imag_out = apply_mna(conduct_dense, vector[1]) + angular * apply_mna(capacit_dense, vector[0]) + jnp.imag(response)
        return jnp.stack([real_out, imag_out])

    return (product(first_vector), product(second_vector))
```

```python
import math

import jax
import jax.numpy as jnp
from jax import lax
from jax.sharding import PartitionSpec as P

precise = lax.Precision.HIGH


def contract(form, left, right):
    return jnp.einsum(form, left, right, precision=precise)


def cos_sin(first, second, length):
    angle = (first[:, None] * second[None, :] % length).astype(jnp.float32) * (
        2.0 * math.pi / length
    )
    return (jnp.cos(angle), jnp.sin(angle))


def body(
    first_vector, second_vector, conductance, terminals, pattern, conduct_blocks, capacit_blocks
):
    freq_count = lax.axis_size("freq")
    groups = lax.axis_size("node")
    local_bins = first_vector.shape[1]
    node_dev = first_vector.shape[2]
    inner_size = first_vector.shape[3]
    outer_size = local_bins * freq_count
    samples = outer_size * inner_size
    local_steps = inner_size // freq_count
    capacity = node_dev // groups
    freq_index = lax.axis_index("freq")
    node_index = lax.axis_index("node")
    bin_first = freq_index * local_bins + jnp.arange(local_bins, dtype=jnp.int32)
    step_first = freq_index * local_steps + jnp.arange(local_steps, dtype=jnp.int32)
    inner_range = jnp.arange(inner_size, dtype=jnp.int32)
    outer_range = jnp.arange(outer_size, dtype=jnp.int32)
    inner_cos, inner_sin = cos_sin(inner_range, inner_range, inner_size)
    outer_cos, outer_sin = cos_sin(outer_range, outer_range, outer_size)
    back_cos, back_sin = cos_sin(inner_range, bin_first, samples)
    fore_cos, fore_sin = cos_sin(step_first, outer_range, samples)

    def wave(cos, sin):
        return jnp.stack(
            [jnp.stack([cos, sin], axis=1), jnp.stack([-sin, cos], axis=1)], axis=0
        )

    inner_back = wave(inner_cos, inner_sin)
    outer_back = wave(outer_cos, outer_sin) / samples
    inner_fore = wave(inner_cos, -inner_sin)
    outer_fore = wave(outer_cos, -outer_sin)

    def inverse_first(vector):
        mixed = contract("canb,cbem->eman", vector, inner_back)
        cos, sin = back_cos[:, :, None], back_sin[:, :, None]
        return jnp.stack(
            [mixed[0] * cos - mixed[1] * sin, mixed[0] * sin + mixed[1] * cos]
        )

    def inverse_exchange(twisted):
        return lax.all_to_all(twisted, "freq", split_axis=1, concat_axis=2, tiled=True)

    def inverse_second(spread):
        return contract("cman,cael->emnl", spread, outer_back)

    def forward_first(current):
        stamped = contract("cmdl,nd->cmnl", current, incidence)
        turned = contract("cmnl,clea->eman", stamped, outer_fore)
        cos, sin = fore_cos[:, :, None], fore_sin[:, :, None]
        return jnp.stack(
            [turned[0] * cos + turned[1] * sin, turned[1] * cos - turned[0] * sin]
        )

    def forward_exchange(twisted):
        return lax.all_to_all(twisted, "freq", split_axis=2, concat_axis=1, tiled=True)

    def forward_second(collected):
        return contract("cman,cmeb->eanb", collected, inner_fore)

    def arrange(values, axis):
        return jnp.concatenate(
            [
                lax.dynamic_slice_in_dim(values, (node_index ^ s) * capacity, capacity, axis)
                for s in range(groups)
            ],
            axis=axis,
        )

    own_rows = arrange(
        lax.dynamic_slice_in_dim(terminals, node_index * node_dev, node_dev, 0), 0
    )
    node_ids = jnp.arange(node_dev, dtype=jnp.int32)
    drain_hot = (node_ids[:, None] == own_rows[None, :, 0]).astype(jnp.float32)
    source_hot = (node_ids[:, None] == own_rows[None, :, 1]).astype(jnp.float32)
    incidence = drain_hot - source_hot
    arranged = terminals.reshape(groups, groups, capacity, 3)
    wanted = lax.dynamic_index_in_dim(arranged, node_index, axis=1, keepdims=False)
    conduct = arrange(conductance, 2)
    trans_g, output_g = conduct[0], conduct[1]

    def middle(signal):
        blocks = []
        for s in range(groups):
            rows = lax.dynamic_index_in_dim(wanted, node_index ^ s, 0, keepdims=False)
            hot = (node_ids[:, None] == rows[None, :, 2]).astype(jnp.float32)
            block = contract("cmnl,np->cmpl", signal, hot)
            if s:
                pairs = [(g, g ^ s) for g in range(groups)]
                block = lax.ppermute(block, "node", pairs)
            blocks.append(block)
        at_source = contract("cmnl,nd->cmdl", signal, source_hot)
        across = contract("cmnl,nd->cmdl", signal, incidence)
        at_gate = jnp.concatenate(blocks, axis=2)
        return trans_g * (at_gate - at_source) + output_g * across

    block_size = conduct_blocks.shape[2]
    block_count = node_dev // block_size
    pattern_hot = (
        pattern[:, :, None] == jnp.arange(block_count, dtype=jnp.int32)[None, None, :]
    ).astype(jnp.float32)

    def dense(blocks):
        return jnp.einsum(
            "bjc,bjrs->brcs", pattern_hot, blocks, precision=lax.Precision.HIGHEST
        ).reshape(node_dev, node_dev)

    conduct_dense = dense(conduct_blocks)
    capacit_dense = dense(capacit_blocks)
    bin_index = bin_first[:, None] + outer_size * inner_range[None, :]
    signed = jnp.where(bin_index < samples // 2, bin_index, bin_index - samples)
    angular = (signed.astype(jnp.float32) * (2.0 * math.pi / samples))[:, None, :]

    def linear(vector):
        real_out = contract("rs,asb->arb", conduct_dense, vector[0]) - angular * contract(
            "rs,asb->arb", capacit_dense, vector[1]
        )
        imag_out = contract("rs,asb->arb", conduct_dense, vector[1]) + angular * contract(
            "rs,asb->arb", capacit_dense, vector[0]
        )
        return jnp.stack([real_out, imag_out])

    twisted_one = inverse_first(first_vector)
    spread_one = inverse_exchange(twisted_one)
    later, _ = lax.optimization_barrier((second_vector, twisted_one))
    twisted_two = inverse_first(later)
    spread_one, twisted_two = lax.optimization_barrier((spread_one, twisted_two))
    spread_two = inverse_exchange(twisted_two)
    sent_one = forward_first(middle(inverse_second(spread_one)))
    spread_two, sent_one = lax.optimization_barrier((spread_two, sent_one))
    collected_one = forward_exchange(sent_one)
    sent_two = forward_first(middle(inverse_second(spread_two)))
    collected_one, sent_two = lax.optimization_barrier((collected_one, sent_two))
    collected_two = forward_exchange(sent_two)
    vector_one, vector_two, collected_one = lax.optimization_barrier(
        (first_vector, second_vector, collected_one)
    )
    first_product = linear(vector_one) + forward_second(collected_one)
    second_linear = linear(vector_two)
    second_product = second_linear + forward_second(collected_two)
    return (first_product, second_product)


def solution(mesh):
    return jax.shard_map(
        body,
        mesh=mesh,
        in_specs=(
            P(None, "freq", "node", None),
            P(None, "freq", "node", None),
            P(None, "freq", "node", None),
            P(),
            P("node", None),
            P("node", None, None, None),
            P("node", None, None, None),
        ),
        out_specs=(P(None, "freq", "node", None), P(None, "freq", "node", None)),
        check_vma=False,
    )
```

```python
import math

import jax
import jax.numpy as jnp
from jax import lax
from jax.experimental import pallas as pl
from jax.experimental.layout import Layout, with_layout_constraint
from jax.experimental.pallas import tpu as pltpu
from jax.sharding import PartitionSpec as P

precise = lax.Precision.HIGH


def contract(form, left, right):
    return jnp.einsum(form, left, right, precision=precise)


def cos_sin(first, second, length):
    angle = (first[:, None] * second[None, :] % length).astype(jnp.float32) * (
        2.0 * math.pi / length
    )
    return (jnp.cos(angle), jnp.sin(angle))


def split(values):
    high = values.astype(jnp.bfloat16)
    low = (values - high.astype(jnp.float32)).astype(jnp.bfloat16)
    return high, low


def dot(left, right):
    return lax.dot_general(
        left, right, (((0,), (0,)), ((), ())), preferred_element_type=jnp.float32
    )


def last_kernel(collected_ref, wave_ref, linear_ref, out_ref, high_ref, low_ref):
    shards, bins, _, steps, nodes = collected_ref.shape
    inner = shards * steps

    @pl.when(pl.program_id(0) == 0)
    def _():
        high, low = split(wave_ref[...])
        high_ref[...] = high
        low_ref[...] = low

    for t in range(0, bins, 2):
        columns = [
            jnp.concatenate(
                [collected_ref[:, u, c].reshape(inner, nodes) for c in range(2)], axis=0
            )
            for u in (t, t + 1)
        ]
        high, low = split(jnp.concatenate(columns, axis=1))
        total = dot(high, low_ref[...]) + dot(low, high_ref[...])
        total = total + dot(high, high_ref[...])
        for h in range(2):
            rows = total[h * nodes : (h + 1) * nodes]
            for e in range(2):
                part = rows[:, e * inner : (e + 1) * inner]
                out_ref[e, t + h] = linear_ref[e, t + h] + part


def last_stage(collected, wave, linear):
    shards, bins, _, steps, nodes = collected.shape
    inner = shards * steps
    tile = 4
    return pl.pallas_call(
        last_kernel,
        grid=(bins // tile,),
        in_specs=[
            pl.BlockSpec((shards, tile, 2, steps, nodes), lambda i: (0, i, 0, 0, 0)),
            pl.BlockSpec((2 * inner, 2 * inner), lambda i: (0, 0)),
            pl.BlockSpec((2, tile, nodes, inner), lambda i: (0, i, 0, 0)),
        ],
        out_specs=pl.BlockSpec((2, tile, nodes, inner), lambda i: (0, i, 0, 0)),
        out_shape=jax.ShapeDtypeStruct(linear.shape, jnp.float32),
        scratch_shapes=[
            pltpu.VMEM((2 * inner, 2 * inner), jnp.bfloat16),
            pltpu.VMEM((2 * inner, 2 * inner), jnp.bfloat16),
        ],
        compiler_params=pltpu.CompilerParams(vmem_limit_bytes=32 * 1024 * 1024),
        cost_estimate=pl.CostEstimate(
            flops=6 * bins * nodes * 4 * inner * inner,
            bytes_accessed=12 * collected.size,
            transcendentals=0,
        ),
    )(collected, wave, linear)


def dot_rows(left, right):
    return lax.dot_general(
        left, right, (((1,), (1,)), ((), ())), preferred_element_type=jnp.float32
    )


def first_kernel(vector_ref, wave_ref, cos_ref, sin_ref, out_ref, high_ref, low_ref):
    _, bins, nodes, inner = vector_ref.shape

    @pl.when(pl.program_id(0) == 0)
    def _():
        high, low = split(wave_ref[...])
        high_ref[...] = high
        low_ref[...] = low

    for t in range(0, bins, 2):
        row = jnp.concatenate(
            [vector_ref[c, t : t + 2].reshape(2 * nodes, inner) for c in range(2)], axis=1
        )
        high, low = split(row)
        total = dot_rows(low_ref[...], high) + dot_rows(high_ref[...], low)
        total = total + dot_rows(high_ref[...], high)
        for h in range(2):
            real = total[:inner, h * nodes : (h + 1) * nodes]
            imag = total[inner:, h * nodes : (h + 1) * nodes]
            cos = cos_ref[0, :, t + h : t + h + 1]
            sin = sin_ref[0, :, t + h : t + h + 1]
            out_ref[:, 0, t + h, :] = real * cos - imag * sin
            out_ref[:, 1, t + h, :] = real * sin + imag * cos


def first_stage(vector, wave, cos, sin):
    _, bins, nodes, inner = vector.shape
    tile = 8
    tiled = [part.reshape(inner, bins // tile, tile).transpose(1, 0, 2) for part in (cos, sin)]
    return pl.pallas_call(
        first_kernel,
        grid=(bins // tile,),
        in_specs=[
            pl.BlockSpec((2, tile, nodes, inner), lambda i: (0, i, 0, 0)),
            pl.BlockSpec((2 * inner, 2 * inner), lambda i: (0, 0)),
            pl.BlockSpec((1, inner, tile), lambda i: (i, 0, 0)),
            pl.BlockSpec((1, inner, tile), lambda i: (i, 0, 0)),
        ],
        out_specs=pl.BlockSpec((inner, 2, tile, nodes), lambda i: (0, 0, i, 0)),
        out_shape=jax.ShapeDtypeStruct((inner, 2, bins, nodes), jnp.float32),
        scratch_shapes=[
            pltpu.VMEM((2 * inner, 2 * inner), jnp.bfloat16),
            pltpu.VMEM((2 * inner, 2 * inner), jnp.bfloat16),
        ],
        compiler_params=pltpu.CompilerParams(vmem_limit_bytes=32 * 1024 * 1024),
        cost_estimate=pl.CostEstimate(
            flops=6 * bins * nodes * 4 * inner * inner,
            bytes_accessed=8 * vector.size,
            transcendentals=0,
        ),
    )(vector, wave, *tiled)


def body(
    first_vector, second_vector, conductance, terminals, pattern, conduct_blocks, capacit_blocks
):
    freq_count = lax.axis_size("freq")
    groups = lax.axis_size("node")
    local_bins = first_vector.shape[1]
    node_dev = first_vector.shape[2]
    inner_size = first_vector.shape[3]
    outer_size = local_bins * freq_count
    samples = outer_size * inner_size
    local_steps = inner_size // freq_count
    capacity = node_dev // groups
    freq_index = lax.axis_index("freq")
    node_index = lax.axis_index("node")
    bin_first = freq_index * local_bins + jnp.arange(local_bins, dtype=jnp.int32)
    step_first = freq_index * local_steps + jnp.arange(local_steps, dtype=jnp.int32)
    inner_range = jnp.arange(inner_size, dtype=jnp.int32)
    outer_range = jnp.arange(outer_size, dtype=jnp.int32)
    inner_cos, inner_sin = cos_sin(inner_range, inner_range, inner_size)
    outer_cos, outer_sin = cos_sin(outer_range, outer_range, outer_size)
    back_cos, back_sin = cos_sin(inner_range, bin_first, samples)
    fore_cos, fore_sin = cos_sin(step_first, outer_range, samples)

    def wave(cos, sin):
        return jnp.stack(
            [jnp.stack([cos, sin], axis=1), jnp.stack([-sin, cos], axis=1)], axis=0
        )

    inner_back = wave(inner_cos, inner_sin)
    outer_back = wave(outer_cos, outer_sin) / samples
    inner_fore = wave(inner_cos, -inner_sin)
    outer_fore = wave(outer_cos, -outer_sin)

    def inverse_first(vector):
        rows = inner_back.transpose(2, 3, 0, 1).reshape(2 * inner_size, 2 * inner_size)
        return first_stage(vector, rows, back_cos, back_sin)

    def inverse_exchange(twisted):
        return lax.all_to_all(twisted, "freq", split_axis=0, concat_axis=0, tiled=True)

    def inverse_second(spread):
        parts = spread.reshape(freq_count, local_steps, 2, local_bins, node_dev)
        joined = parts.transpose(2, 1, 0, 3, 4).reshape(
            2, local_steps, outer_size, node_dev
        )
        return contract("cman,cael->emnl", joined, outer_back)

    def forward_first(current):
        stamped = contract("cmdl,nd->cmnl", current, incidence)
        turned = contract("cmnl,clea->eamn", stamped, outer_fore)
        cos, sin = fore_cos.T[:, :, None], fore_sin.T[:, :, None]
        twisted = jnp.stack(
            [turned[0] * cos + turned[1] * sin, turned[1] * cos - turned[0] * sin], axis=1
        )
        return with_layout_constraint(twisted, Layout(major_to_minor=(0, 1, 2, 3)))

    def forward_exchange(twisted):
        return lax.all_to_all(twisted, "freq", split_axis=0, concat_axis=0, tiled=True)

    def forward_second(collected, linear_part):
        parts = collected.reshape(freq_count, local_bins, 2, local_steps, node_dev)
        return last_stage(
            parts, inner_fore.reshape(2 * inner_size, 2 * inner_size), linear_part
        )

    def arrange(values, axis):
        return jnp.concatenate(
            [
                lax.dynamic_slice_in_dim(values, (node_index ^ s) * capacity, capacity, axis)
                for s in range(groups)
            ],
            axis=axis,
        )

    own_rows = arrange(
        lax.dynamic_slice_in_dim(terminals, node_index * node_dev, node_dev, 0), 0
    )
    node_ids = jnp.arange(node_dev, dtype=jnp.int32)
    drain_hot = (node_ids[:, None] == own_rows[None, :, 0]).astype(jnp.float32)
    source_hot = (node_ids[:, None] == own_rows[None, :, 1]).astype(jnp.float32)
    incidence = drain_hot - source_hot
    arranged = terminals.reshape(groups, groups, capacity, 3)
    wanted = lax.dynamic_index_in_dim(arranged, node_index, axis=1, keepdims=False)
    conduct = arrange(conductance, 2)
    trans_g, output_g = conduct[0], conduct[1]

    def middle(signal):
        blocks = []
        for s in range(groups):
            rows = lax.dynamic_index_in_dim(wanted, node_index ^ s, 0, keepdims=False)
            hot = (node_ids[:, None] == rows[None, :, 2]).astype(jnp.float32)
            block = contract("cmnl,np->cmpl", signal, hot)
            if s:
                pairs = [(g, g ^ s) for g in range(groups)]
                block = lax.ppermute(block, "node", pairs)
            blocks.append(block)
        at_source = contract("cmnl,nd->cmdl", signal, source_hot)
        across = contract("cmnl,nd->cmdl", signal, incidence)
        at_gate = jnp.concatenate(blocks, axis=2)
        return trans_g * (at_gate - at_source) + output_g * across

    block_size = conduct_blocks.shape[2]
    block_count = node_dev // block_size
    pattern_hot = (
        pattern[:, :, None] == jnp.arange(block_count, dtype=jnp.int32)[None, None, :]
    ).astype(jnp.float32)

    def dense(blocks):
        return jnp.einsum(
            "bjc,bjrs->brcs", pattern_hot, blocks, precision=lax.Precision.HIGHEST
        ).reshape(node_dev, node_dev)

    conduct_dense = dense(conduct_blocks)
    capacit_dense = dense(capacit_blocks)
    bin_index = bin_first[:, None] + outer_size * inner_range[None, :]
    signed = jnp.where(bin_index < samples // 2, bin_index, bin_index - samples)
    angular = (signed.astype(jnp.float32) * (2.0 * math.pi / samples))[:, None, :]

    def linear(vector):
        real_out = contract("rs,asb->arb", conduct_dense, vector[0]) - angular * contract(
            "rs,asb->arb", capacit_dense, vector[1]
        )
        imag_out = contract("rs,asb->arb", conduct_dense, vector[1]) + angular * contract(
            "rs,asb->arb", capacit_dense, vector[0]
        )
        return jnp.stack([real_out, imag_out])

    twisted_one = inverse_first(first_vector)
    spread_one = inverse_exchange(twisted_one)
    later, _ = lax.optimization_barrier((second_vector, twisted_one))
    twisted_two = inverse_first(later)
    spread_one, twisted_two = lax.optimization_barrier((spread_one, twisted_two))
    spread_two = inverse_exchange(twisted_two)
    sent_one = forward_first(middle(inverse_second(spread_one)))
    spread_two, sent_one = lax.optimization_barrier((spread_two, sent_one))
    collected_one = forward_exchange(sent_one)
    sent_two = forward_first(middle(inverse_second(spread_two)))
    collected_one, sent_two = lax.optimization_barrier((collected_one, sent_two))
    collected_two = forward_exchange(sent_two)
    vector_one, vector_two, collected_one = lax.optimization_barrier(
        (first_vector, second_vector, collected_one)
    )
    first_product = forward_second(collected_one, linear(vector_one))
    second_product = forward_second(collected_two, linear(vector_two))
    return (first_product, second_product)


def solution(mesh):
    return jax.shard_map(
        body,
        mesh=mesh,
        in_specs=(
            P(None, "freq", "node", None),
            P(None, "freq", "node", None),
            P(None, "freq", "node", None),
            P(),
            P("node", None),
            P("node", None, None, None),
            P("node", None, None, None),
        ),
        out_specs=(P(None, "freq", "node", None), P(None, "freq", "node", None)),
        check_vma=False,
    )
```
